512 devices in a mesh: par: 64 (over x, z), obs: 8 (over y, core).
Axes of the slice: x: 4, y: 4, z: 16, core: 2. Of those that a mesh axis runs over, the one named last changes fastest.
Arguments:
- unscaled_tile_values: bfloat16 [128, 8, 1024, 1024], P('par', 'obs'), may hold values from -0.046875 to 0.046875
- tile_observe_row: int32 [128, 8], P('par', 'obs'), may hold values from 0 to 1
- tile_param_block: int32 [128, 8], P('par', 'obs'), may hold values from 0 to 1
- tile_scale_exponent: int32 [128, 8], P('par', 'obs'), may hold values from -1 to 2
- tile_count: int32 [64, 8], P('par', 'obs'), may hold values from 0 to 2, as said below
- probes: bfloat16 [131072, 64], P(('par', 'obs')), may hold values from -6 to 6
- noise_weight: float32 [16384], P('obs'), may hold values from 0.25 to 4
Outputs:
- range_basis: float32 [131072, 64], P(('par', 'obs'))
The draws below stay inside these ranges and needn't reach their ends.
Inputs may be any that keep to these rules, and one draw needn't show every extreme that they name: `tile_count`: some device has all 2 slots live in every draw; many have none.
All inputs are finite; a program needn't handle non-finite values.
Results may differ from the reference program's by a relative error of at most 0.0027.
Values may be sent and summed in bfloat16 or wider, within the bound.
No kernel may reach another device: no remote copies, remote signals or barrier semaphores. Data moves between devices by JAX's collectives and lax.ppermute only.
A program may use at most 64 MiB of HBM per device.

```python
import math
import jax
import jax.numpy as jnp
from jax import lax

TILE_EXTENT = 1024
PROBES = 64
PARAM_BLOCKS = 2
OBSERVE_TILE_ROWS = 2
K_DEV = 2
NOBS = 16384
NPARAM = 131072
SLOT_COUNT = 128
N_PAR = 64
N_OBS = 8


def draw_tile_count(key, part):
    key = jax.random.fold_in(key, 7)
    first_key, second_key = jax.random.split(key)
    levels = jax.random.randint(first_key, (N_PAR * N_OBS,), 0, 10)
    counts = ((levels >= 5).astype(jnp.int32) + (levels >= 8).astype(jnp.int32)) * K_DEV // 2
    picked = jax.random.randint(second_key, (), 0, N_PAR * N_OBS)
    counts = counts.at[picked].set(K_DEV)
    return counts.reshape(N_PAR, N_OBS).astype(jnp.int32)


def set_ends(array, key, low, high):
    longest = array.shape.index(max(array.shape))
    spots = []
    for shift in (0, 1):
        where = [jax.random.randint(jax.random.fold_in(key, axis), (), 0, length) for axis, length in enumerate(array.shape)]
        where[longest] = (where[longest] + shift) % array.shape[longest]
        spots.append(tuple(where))
    return array.at[spots[0]].set(low).at[spots[1]].set(high)


def shard_levels(rng, dims, cuts, least, top_value):
    gain = 1.0
    for position, shards_of in cuts:
        steps = jax.random.uniform(jax.random.fold_in(jax.random.fold_in(rng, 6), position), (shards_of,), jnp.float32, least / len(cuts), top_value / len(cuts))
        gain = gain * jnp.repeat(jnp.exp(steps), dims[position] // shards_of).reshape((-1,) + (1,) * (len(dims) - 1 - position))
    return gain


def normal_values(own_key, dims, spread, most, pieces=(), held_as=jnp.bfloat16):
    loudness = shard_levels(own_key, dims, pieces, -0.22, 0.18) if pieces else 1.0
    drawn = jax.random.normal(own_key, dims, jnp.float32) * spread * loudness
    return jnp.minimum(jnp.maximum(drawn, -most), most).astype(held_as)


def setup_inputs(seed: int = 0) -> dict:
    seeds = jax.random.split(jax.random.key(seed), 8)
    return {
        "unscaled_tile_values": normal_values(seeds[0], (SLOT_COUNT, N_OBS, TILE_EXTENT, TILE_EXTENT), (TILE_EXTENT * N_PAR // (2 * OBSERVE_TILE_ROWS)) ** -0.5, 0.046875, ((0, 64), (1, 8))),
        "tile_observe_row": set_ends(jax.random.randint(seeds[1], (SLOT_COUNT, N_OBS), 0, OBSERVE_TILE_ROWS), jax.random.fold_in(seeds[1], 1), 0, OBSERVE_TILE_ROWS - 1).astype(jnp.int32),
        "tile_param_block": set_ends(jax.random.randint(seeds[2], (SLOT_COUNT, N_OBS), 0, PARAM_BLOCKS), jax.random.fold_in(seeds[2], 1), 0, PARAM_BLOCKS - 1).astype(jnp.int32),
        "tile_scale_exponent": set_ends(jax.random.randint(seeds[3], (SLOT_COUNT, N_OBS), -1, 3), jax.random.fold_in(seeds[3], 1), -1, 2).astype(jnp.int32),
        "tile_count": draw_tile_count(jax.random.fold_in(seeds[7], 71), 0),
        "probes": normal_values(seeds[5], (NPARAM, PROBES), 1.0, 6.0, ((0, 512),)),
        "noise_weight": jnp.clip(jnp.exp(math.log(4.0) - 2.7725887 * jax.random.uniform(seeds[6], (NOBS,), jnp.float32) ** shard_levels(seeds[6], (NOBS,), ((0, 8),), -0.2, 0.2)), 0.25, 4.0),
    }


def reference(unscaled_tile_values, tile_observe_row, tile_param_block, tile_scale_exponent, tile_count, probes, noise_weight):
    overall_count = SLOT_COUNT * N_OBS

    def tile_info(index):
        slot = index // N_OBS
        block = index % N_OBS
        group = slot // K_DEV
        kslot = slot % K_DEV
        live = kslot < tile_count[group, block]
        scale = jnp.exp2(tile_scale_exponent[slot, block].astype(jnp.float32))
        row_start = ((block * OBSERVE_TILE_ROWS + tile_observe_row[slot, block]) * TILE_EXTENT).astype(jnp.int32)
        col_start = ((group * PARAM_BLOCKS + tile_param_block[slot, block]) * TILE_EXTENT).astype(jnp.int32)
        return unscaled_tile_values[slot, block], live, scale, row_start, col_start

    def forward_step(index, forward):
        matrix, live, scale, row_start, col_start = tile_info(index)
        panel = lax.dynamic_slice_in_dim(probes, col_start, TILE_EXTENT, 0)
        product = jnp.dot(matrix, panel, preferred_element_type=jnp.float32) * scale
        product = jnp.where(live, product, jnp.zeros_like(product))
        current = lax.dynamic_slice_in_dim(forward, row_start, TILE_EXTENT, 0)
        return lax.dynamic_update_slice_in_dim(forward, current + product, row_start, 0)

    forward = lax.fori_loop(0, overall_count, forward_step, jnp.zeros((NOBS, PROBES), jnp.float32))
    weighted = (noise_weight[:, None] * forward).astype(jnp.bfloat16)

    def back_step(index, result):
        matrix, live, scale, row_start, col_start = tile_info(index)
        rows = lax.dynamic_slice_in_dim(weighted, row_start, TILE_EXTENT, 0)
        product = jnp.dot(matrix.T, rows, preferred_element_type=jnp.float32) * scale
        product = jnp.where(live, product, jnp.zeros_like(product))
        current = lax.dynamic_slice_in_dim(result, col_start, TILE_EXTENT, 0)
        return lax.dynamic_update_slice_in_dim(result, current + product, col_start, 0)

    return lax.fori_loop(0, overall_count, back_step, jnp.zeros((NPARAM, PROBES), jnp.float32))
```

```python
import jax
import jax.numpy as jnp
from jax import lax
from jax.sharding import Mesh, PartitionSpec as P

OBS = ("y", "core")
PAR = ("x", "zh", "zl")
NEAR = ("x", "zl")


def exchange(pieces, axes):
    return lax.all_to_all(pieces, axes, 0, 0, tiled=True)


def shards(
    unscaled_tile_values,
    tile_observe_row,
    tile_param_block,
    tile_scale_exponent,
    tile_count,
    probes,
    noise_weight,
):
    slots = unscaled_tile_values.shape[0]
    side = unscaled_tile_values.shape[-1]
    own, width = probes.shape
    n_obs = lax.axis_size(OBS)
    n_near = lax.axis_size(NEAR)
    obs_rows = noise_weight.shape[0]
    piece = obs_rows // n_near
    live_count = tile_count[0, 0]

    panels = exchange(jnp.broadcast_to(probes.T, (n_obs, width, own)), OBS)
    panels = panels.transpose(1, 0, 2).reshape(width, n_obs * own)

    forward = jnp.zeros((width, obs_rows), jnp.float32)
    for k in range(slots):
        scale = jnp.exp2(tile_scale_exponent[k, 0].astype(jnp.float32))
        row = tile_observe_row[k, 0] * side
        col = tile_param_block[k, 0] * side

        def live_product(k=k, col=col, scale=scale):
            panel = lax.dynamic_slice_in_dim(panels, col, side, 1)
            return scale * lax.dot_general(
                panel,
                unscaled_tile_values[k, 0],
                (((1,), (1,)), ((), ())),
                preferred_element_type=jnp.float32,
            )

        def dead_product():
            return jnp.zeros((width, side), jnp.float32)

        product = lax.cond(k < live_count, live_product, dead_product)
        current = lax.dynamic_slice_in_dim(forward, row, side, 1)
        forward = lax.dynamic_update_slice_in_dim(forward, current + product, row, 1)

    pieces = forward.reshape(width, n_near, piece).transpose(1, 0, 2)
    partial = exchange(pieces, NEAR).sum(0)
    total = lax.all_gather(partial, "zh").sum(0)
    here = lax.axis_index(NEAR)
    noise = lax.dynamic_slice_in_dim(noise_weight, here * piece, piece, 0)
    part = (noise[None, :] * total).astype(jnp.bfloat16)
    weighted = exchange(jnp.broadcast_to(part, (n_near, width, piece)), NEAR)
    weighted = weighted.transpose(1, 0, 2).reshape(width, obs_rows)

    result = jnp.zeros((width, n_obs * own), jnp.float32)
    for k in range(slots):
        scale = jnp.exp2(tile_scale_exponent[k, 0].astype(jnp.float32))
        row = tile_observe_row[k, 0] * side
        col = tile_param_block[k, 0] * side

        def live_back(k=k, row=row, scale=scale):
            rows = lax.dynamic_slice_in_dim(weighted, row, side, 1)
            return scale * jnp.dot(
                rows, unscaled_tile_values[k, 0], preferred_element_type=jnp.float32
            )

        def dead_back():
            return jnp.zeros((width, side), jnp.float32)

        product = lax.cond(k < live_count, live_back, dead_back)
        current = lax.dynamic_slice_in_dim(result, col, side, 1)
        result = lax.dynamic_update_slice_in_dim(result, current + product, col, 1)
    pieces = result.astype(jnp.bfloat16).reshape(width, n_obs, own).transpose(1, 0, 2)
    summed = exchange(pieces, OBS).astype(jnp.float32).sum(0)
    return summed.T


def solution(mesh):
    near = 4
    n_par, n_obs = mesh.devices.shape
    n_x = 4
    devices = mesh.devices.reshape(n_x, n_par // n_x // near, near, n_obs // 2, 2)
    split = Mesh(devices, PAR + OBS)
    in_specs = (
        P(PAR, OBS, None, None),
        P(PAR, OBS),
        P(PAR, OBS),
        P(PAR, OBS),
        P(PAR, OBS),
        P(PAR + OBS, None),
        P(OBS),
    )
    out_specs = P(PAR + OBS, None)
    return jax.shard_map(shards, mesh=split, in_specs=in_specs, out_specs=out_specs, check_vma=False)
```

```python
import jax
import jax.numpy as jnp
from jax import lax
from jax.experimental import pallas as pl
from jax.experimental.pallas import tpu as pltpu
from jax.sharding import Mesh, PartitionSpec as P

OBS = ("y", "core")
PAR = ("x", "zh", "zl")
NEAR = ("x", "zl")
VMEM = pl.BlockSpec(memory_space=pltpu.VMEM)
SMEM = pl.BlockSpec(memory_space=pltpu.SMEM)
HBM = pl.BlockSpec(memory_space=pltpu.HBM)
PARAMS = pltpu.CompilerParams(vmem_limit_bytes=32 * 2**20)
BAND = 256


def exchange(pieces, axes):
    return lax.all_to_all(pieces, axes, 0, 0, tiled=True)


def in_hbm(array):
    return pltpu.with_memory_space_constraint(array, pltpu.HBM)


def call(kernel, out, in_specs, *args, out_specs=VMEM, scratch=()):
    return pl.pallas_call(
        kernel,
        out_shape=out,
        in_specs=in_specs,
        out_specs=out_specs,
        scratch_shapes=list(scratch),
        compiler_params=PARAMS,
    )(*args)


def power(exponent):
    return lax.shift_left(jnp.int32(1), exponent + 1).astype(jnp.float32) * 0.5


def start_kernel(count, row, col, exponent, probes, copies, info, arrived):
    sent = [
        pltpu.make_async_copy(probes, copies.at[i], arrived.at[i]) for i in range(copies.shape[0])
    ]
    for copy in sent:
        copy.start()
    slots = row.shape[1]
    info[0] = count[0, 0]
    for k in range(slots):
        info[1 + k] = row[0, k]
        info[1 + slots + k] = col[0, k]
        info[1 + 2 * slots + k] = exponent[0, k]
    for copy in sent:
        copy.wait()


def slot_info(info, k, slots):
    scale = power(info[1 + 2 * slots + k])
    return k < info[0], info[1 + k], info[1 + slots + k], scale


def load_bands(tiles, held, arrived):
    slots, _, side, _ = tiles.shape
    loads = {}
    for k in range(slots):
        for j in range(side // BAND):
            band = pl.ds(BAND * j, BAND)
            loads[k, j] = pltpu.make_async_copy(
                tiles.at[k, 0, band], held.at[k, band], arrived.at[k, j]
            )
            loads[k, j].start()
    return loads


def forward_kernel(info, panels, tiles, out, held, arrived):
    loads = load_bands(tiles, held, arrived)
    slots, side, _ = held.shape
    own, piece = panels.shape[2], out.shape[2]
    per_col, per_row, per_band = side // own, side // piece, BAND // piece
    out[...] = jnp.zeros_like(out)
    for k in range(slots):
        live, row, col, scale = slot_info(info, k, slots)
        for j in range(side // BAND):
            loads[k, j].wait()

            @pl.when(live)
            def _(j=j, k=k, row=row, col=col, scale=scale):
                panel = jnp.concatenate([panels[col * per_col + i] for i in range(per_col)], axis=1)
                product = scale * lax.dot_general(
                    panel,
                    held[k, pl.ds(BAND * j, BAND), :],
                    (((1,), (1,)), ((), ())),
                    preferred_element_type=jnp.float32,
                )
                for t in range(per_band):
                    where = row * per_row + j * per_band + t
                    out[where] = out[where] + product[:, t * piece : (t + 1) * piece]


def weigh_kernel(sums, noise, out):
    here = lax.axis_index(NEAR)
    total = sums[0]
    for i in range(1, sums.shape[0]):
        total = total + sums[i]
    weighted = (noise[pl.ds(here, 1), :] * total).astype(jnp.bfloat16)
    for i in range(out.shape[0]):
        out[i] = weighted


def back_kernel(info, weighted, tiles, out, total, held, arrived):
    loads = load_bands(tiles, held, arrived)
    slots, side, _ = held.shape
    piece, own = weighted.shape[2], out.shape[2]
    per_col, per_row, per_band = side // own, side // piece, BAND // piece
    total[...] = jnp.zeros_like(total)
    for k in range(slots):
        live, row, col, scale = slot_info(info, k, slots)
        for j in range(side // BAND):
            loads[k, j].wait()

            @pl.when(live)
            def _(j=j, k=k, row=row, col=col, scale=scale):
                first = row * per_row + j * per_band
                rows = jnp.concatenate([weighted[first + i] for i in range(per_band)], axis=1)
                product = scale * jnp.dot(
                    rows,
                    held[k, pl.ds(BAND * j, BAND), :],
                    preferred_element_type=jnp.float32,
                )
                for t in range(per_col):
                    where = col * per_col + t
                    total[where] = total[where] + product[:, t * own : (t + 1) * own]

    out[...] = total[...].astype(jnp.bfloat16)


def shards(
    unscaled_tile_values,
    tile_observe_row,
    tile_param_block,
    tile_scale_exponent,
    tile_count,
    probes,
    noise_weight,
):
    own, width = probes.shape
    n_obs = lax.axis_size(OBS)
    n_near = lax.axis_size(NEAR)
    piece = noise_weight.shape[0] // n_near
    slots, _, side, _ = unscaled_tile_values.shape
    bf16, f32 = jnp.bfloat16, jnp.float32

    copies, info = call(
        start_kernel,
        (pltpu.VMEM((n_obs, width, own), bf16), pltpu.SMEM((1 + 3 * slots,), jnp.int32)),
        [SMEM] * 4 + [HBM],
        tile_count,
        in_hbm(tile_observe_row.T),
        in_hbm(tile_param_block.T),
        in_hbm(tile_scale_exponent.T),
        in_hbm(probes.T),
        out_specs=(VMEM, SMEM),
        scratch=[pltpu.SemaphoreType.DMA((n_obs,))],
    )
    panels = exchange(copies, OBS)
    bands = [
        pltpu.VMEM((slots, side, side), bf16),
        pltpu.SemaphoreType.DMA((slots, side // BAND)),
    ]
    pieces = call(
        forward_kernel,
        pltpu.VMEM((n_near, width, piece), f32),
        [SMEM, VMEM, HBM],
        info,
        panels,
        in_hbm(unscaled_tile_values),
        scratch=bands,
    )
    partial = exchange(pieces, NEAR).sum(0)
    sums = lax.all_gather(partial, "zh")
    weighted = call(
        weigh_kernel,
        pltpu.VMEM((n_near, width, piece), bf16),
        [VMEM] * 2,
        sums,
        noise_weight.reshape(n_near, piece),
    )
    weighted = exchange(weighted, NEAR)
    pieces = call(
        back_kernel,
        pltpu.VMEM((n_obs, width, own), bf16),
        [SMEM, VMEM, HBM],
        info,
        weighted,
        in_hbm(unscaled_tile_values),
        scratch=[pltpu.VMEM((n_obs, width, own), f32)] + bands,
    )
    summed = exchange(pieces, OBS).astype(f32).sum(0)
    return summed.T


def solution(mesh):
    n_par, n_obs = mesh.devices.shape
    devices = mesh.devices.reshape(4, n_par // 16, 4, n_obs // 2, 2)
    split = Mesh(devices, PAR + OBS)
    in_specs = (
        P(PAR, OBS, None, None),
        P(PAR, OBS),
        P(PAR, OBS),
        P(PAR, OBS),
        P(PAR, OBS),
        P(PAR + OBS, None),
        P(OBS),
    )
    out_specs = P(PAR + OBS, None)
    return jax.shard_map(shards, mesh=split, in_specs=in_specs, out_specs=out_specs, check_vma=False)
```

```python
import jax
import jax.numpy as jnp
from jax import lax
from jax.experimental import pallas as pl
from jax.experimental.pallas import tpu as pltpu
from jax.sharding import Mesh, PartitionSpec as P

OBS = ("y", "core")
PAR = ("x", "zh", "zl")
NEAR = ("x", "zl")
VMEM = pl.BlockSpec(memory_space=pltpu.VMEM)
SMEM = pl.BlockSpec(memory_space=pltpu.SMEM)
HBM = pl.BlockSpec(memory_space=pltpu.HBM)
PARAMS = pltpu.CompilerParams(vmem_limit_bytes=32 * 2**20)
BAND = 256
CODE = jnp.int16
SCALE_ROWS = 16


def exchange(pieces, axes):
    return lax.all_to_all(pieces, axes, 0, 0, tiled=True)


def in_hbm(array):
    return pltpu.with_memory_space_constraint(array, pltpu.HBM)


def call(kernel, out, in_specs, *args, out_specs=VMEM, scratch=()):
    return pl.pallas_call(
        kernel,
        out_shape=out,
        in_specs=in_specs,
        out_specs=out_specs,
        scratch_shapes=list(scratch),
        compiler_params=PARAMS,
    )(*args)


def power(exponent):
    return lax.shift_left(jnp.int32(1), exponent + 1).astype(jnp.float32) * 0.5


def start_kernel(count, row, col, exponent, probes, copies, info, held, arrived, read):
    sent = [
        pltpu.make_async_copy(probes, copies.at[i], arrived.at[i]) for i in range(copies.shape[0])
    ]
    sent += [
        pltpu.make_async_copy(source, held.at[i], read.at[i])
        for i, source in enumerate((row, col, exponent))
    ]
    for copy in sent:
        copy.start()
    for copy in sent:
        copy.wait()
    slots = row.shape[1]
    info[0] = count[0, 0]
    for i in range(3):
        for k in range(slots):
            info[1 + i * slots + k] = held[i, 0, k]


def encode(values, out, at):
    rows = values.shape[0]
    largest = jnp.max(jnp.abs(values), axis=0, keepdims=True)
    exponent = jnp.floor(jnp.log2(jnp.maximum(largest, 2.0**-110))) + 1.0
    codes = jnp.round(values * jnp.exp2(14.0 - exponent))
    out[(*at, pl.ds(0, rows))] = codes.astype(jnp.int32).astype(CODE)
    exponent = jnp.broadcast_to(exponent, (SCALE_ROWS, values.shape[1]))
    out[(*at, pl.ds(rows, SCALE_ROWS))] = exponent.astype(jnp.int32).astype(CODE)


def decode(coded):
    pieces, rows, _ = coded.shape
    rows -= SCALE_ROWS
    total = None
    for i in range(pieces):
        exponent = coded[i, pl.ds(rows, SCALE_ROWS)].astype(jnp.float32)[:1]
        part = coded[i, pl.ds(0, rows)].astype(jnp.float32) * jnp.exp2(exponent - 14.0)
        total = part if total is None else total + part
    return total


def slot_info(info, k, slots):
    scale = power(info[1 + 2 * slots + k])
    return k < info[0], info[1 + k], info[1 + slots + k], scale


def load_bands(tiles, held, arrived):
    slots, _, side, _ = tiles.shape
    loads = {}
    for k in range(slots):
        for j in range(side // BAND):
            band = pl.ds(BAND * j, BAND)
            loads[k, j] = pltpu.make_async_copy(
                tiles.at[k, 0, band], held.at[k, band], arrived.at[k, j]
            )
            loads[k, j].start()
    return loads


def forward_kernel(info, panels, tiles, out, total, held, arrived):
    loads = load_bands(tiles, held, arrived)
    slots, side, _ = held.shape
    own, piece = panels.shape[2], out.shape[2]
    per_col, per_row, per_band = side // own, side // piece, BAND // piece
    total[...] = jnp.zeros_like(total)
    for k in range(slots):
        live, row, col, scale = slot_info(info, k, slots)
        for j in range(side // BAND):
            loads[k, j].wait()

            @pl.when(live)
            def _(j=j, k=k, row=row, col=col, scale=scale):
                panel = jnp.concatenate([panels[col * per_col + i] for i in range(per_col)], axis=1)
                product = scale * lax.dot_general(
                    panel,
                    held[k, pl.ds(BAND * j, BAND), :],
                    (((1,), (1,)), ((), ())),
                    preferred_element_type=jnp.float32,
                )
                for t in range(per_band):
                    where = row * per_row + j * per_band + t
                    total[where] = total[where] + product[:, t * piece : (t + 1) * piece]

    for c in range(out.shape[0]):
        encode(total[c], out, (c,))


def partial_kernel(coded, out):
    encode(decode(coded), out, ())


def weigh_kernel(coded, noise, out):
    here = lax.axis_index(NEAR)
    weighted = (noise[pl.ds(here, 1), :] * decode(coded)).astype(jnp.bfloat16)
    for i in range(out.shape[0]):
        out[i] = weighted


def back_kernel(info, weighted, tiles, out, total, held, arrived):
    loads = load_bands(tiles, held, arrived)
    slots, side, _ = held.shape
    piece, own = weighted.shape[2], out.shape[2]
    per_col, per_row, per_band = side // own, side // piece, BAND // piece
    total[...] = jnp.zeros_like(total)
    for k in range(slots):
        live, row, col, scale = slot_info(info, k, slots)
        for j in range(side // BAND):
            loads[k, j].wait()

            @pl.when(live)
            def _(j=j, k=k, row=row, col=col, scale=scale):
                first = row * per_row + j * per_band
                rows = jnp.concatenate([weighted[first + i] for i in range(per_band)], axis=1)
                product = scale * jnp.dot(
                    rows,
                    held[k, pl.ds(BAND * j, BAND), :],
                    preferred_element_type=jnp.float32,
                )
                for t in range(per_col):
                    where = col * per_col + t
                    total[where] = total[where] + product[:, t * own : (t + 1) * own]

    out[...] = total[...].astype(jnp.bfloat16)


def shards(
    unscaled_tile_values,
    tile_observe_row,
    tile_param_block,
    tile_scale_exponent,
    tile_count,
    probes,
    noise_weight,
):
    own, width = probes.shape
    n_obs = lax.axis_size(OBS)
    n_near = lax.axis_size(NEAR)
    piece = noise_weight.shape[0] // n_near
    slots, _, side, _ = unscaled_tile_values.shape
    bf16, f32 = jnp.bfloat16, jnp.float32

    copies, info = call(
        start_kernel,
        (pltpu.VMEM((n_obs, width, own), bf16), pltpu.SMEM((1 + 3 * slots,), jnp.int32)),
        [SMEM] + [HBM] * 4,
        tile_count,
        in_hbm(tile_observe_row.T),
        in_hbm(tile_param_block.T),
        in_hbm(tile_scale_exponent.T),
        in_hbm(probes.T),
        out_specs=(VMEM, SMEM),
        scratch=[
            pltpu.SMEM((3, 1, slots), jnp.int32),
            pltpu.SemaphoreType.DMA((n_obs,)),
            pltpu.SemaphoreType.DMA((3,)),
        ],
    )
    panels = exchange(copies, OBS)
    bands = [
        pltpu.VMEM((slots, side, side), bf16),
        pltpu.SemaphoreType.DMA((slots, side // BAND)),
    ]
    coded = width + SCALE_ROWS
    pieces = call(
        forward_kernel,
        pltpu.VMEM((n_near, coded, piece), CODE),
        [SMEM, VMEM, HBM],
        info,
        panels,
        in_hbm(unscaled_tile_values),
        scratch=[pltpu.VMEM((n_near, width, piece), f32)] + bands,
    )
    partial = call(
        partial_kernel, pltpu.VMEM((coded, piece), CODE), [VMEM], exchange(pieces, NEAR)
    )
    weighted = call(
        weigh_kernel,
        pltpu.VMEM((n_near, width, piece), bf16),
        [VMEM] * 2,
        lax.all_gather(partial, "zh"),
        noise_weight.reshape(n_near, piece),
    )
    weighted = exchange(weighted, NEAR)
    pieces = call(
        back_kernel,
        pltpu.VMEM((n_obs, width, own), bf16),
        [SMEM, VMEM, HBM],
        info,
        weighted,
        in_hbm(unscaled_tile_values),
        scratch=[pltpu.VMEM((n_obs, width, own), f32)] + bands,
    )
    summed = exchange(pieces, OBS).astype(f32).sum(0)
    return summed.T


def solution(mesh):
    n_par, n_obs = mesh.devices.shape
    devices = mesh.devices.reshape(4, n_par // 16, 4, n_obs // 2, 2)
    split = Mesh(devices, PAR + OBS)
    in_specs = (
        P(PAR, OBS, None, None),
        P(PAR, OBS),
        P(PAR, OBS),
        P(PAR, OBS),
        P(PAR, OBS),
        P(PAR + OBS, None),
        P(OBS),
    )
    out_specs = P(PAR + OBS, None)
    return jax.shard_map(shards, mesh=split, in_specs=in_specs, out_specs=out_specs, check_vma=False)
```

```python
import jax
import jax.numpy as jnp
from jax import lax
from jax.experimental import pallas as pl
from jax.experimental.pallas import tpu as pltpu
from jax.sharding import Mesh, PartitionSpec as P

OBS = ("y", "core")
PAR = ("x", "zh", "zl")
NEAR = ("x", "zl")
VMEM = pl.BlockSpec(memory_space=pltpu.VMEM)
SMEM = pl.BlockSpec(memory_space=pltpu.SMEM)
HBM = pl.BlockSpec(memory_space=pltpu.HBM)
PARAMS = pltpu.CompilerParams(vmem_limit_bytes=16 * 2**20)
BAND = 256
CODE = jnp.int16
SCALE_ROWS = 16


def exchange(pieces, axes):
    return lax.all_to_all(pieces, axes, 0, 0, tiled=True)


def in_hbm(array):
    return pltpu.with_memory_space_constraint(array, pltpu.HBM)


def call(kernel, out, in_specs, *args, out_specs=VMEM, scratch=()):
    return pl.pallas_call(
        kernel,
        out_shape=out,
        in_specs=in_specs,
        out_specs=out_specs,
        scratch_shapes=list(scratch),
        compiler_params=PARAMS,
    )(*args)


def power(exponent):
    return lax.shift_left(jnp.int32(1), exponent + 1).astype(jnp.float32) * 0.5


def start_kernel(count, row, col, exponent, probes, copies, info, held, arrived, read):
    sent = [
        pltpu.make_async_copy(probes, copies.at[i], arrived.at[i]) for i in range(copies.shape[0])
    ]
    sent += [
        pltpu.make_async_copy(source, held.at[i], read.at[i])
        for i, source in enumerate((row, col, exponent))
    ]
    for copy in sent:
        copy.start()
    for copy in sent:
        copy.wait()
    slots = row.shape[1]
    info[0] = count[0, 0]
    for i in range(3):
        for k in range(slots):
            info[1 + i * slots + k] = held[i, 0, k]


def encode(values, out, at):
    rows = values.shape[0]
    largest = jnp.max(jnp.abs(values), axis=0, keepdims=True)
    exponent = jnp.floor(jnp.log2(jnp.maximum(largest, 2.0**-110))) + 1.0
    codes = jnp.round(values * jnp.exp2(14.0 - exponent))
    out[(*at, pl.ds(0, rows))] = codes.astype(jnp.int32).astype(CODE)
    exponent = jnp.broadcast_to(exponent, (SCALE_ROWS, values.shape[1]))
    out[(*at, pl.ds(rows, SCALE_ROWS))] = exponent.astype(jnp.int32).astype(CODE)


def decode(coded):
    pieces, rows, _ = coded.shape
    rows -= SCALE_ROWS
    total = None
    for i in range(pieces):
        exponent = coded[i, pl.ds(rows, SCALE_ROWS)].astype(jnp.float32)[:1]
        part = coded[i, pl.ds(0, rows)].astype(jnp.float32) * jnp.exp2(exponent - 14.0)
        total = part if total is None else total + part
    return total


def slot_info(info, k, slots):
    scale = power(info[1 + 2 * slots + k])
    return k < info[0], info[1 + k], info[1 + slots + k], scale


def load_bands(tiles, held, arrived):
    slots, _, side, _ = tiles.shape
    loads = {}
    for k in range(slots):
        for j in range(side // BAND):
            band = pl.ds(BAND * j, BAND)
            loads[k, j] = pltpu.make_async_copy(
                tiles.at[k, 0, band], held.at[k, band], arrived.at[k, j]
            )
            loads[k, j].start()
    return loads


def forward_kernel(info, panels, tiles, out, held, total, arrived):
    loads = load_bands(tiles, held, arrived)
    slots, side, _ = held.shape
    own, piece = panels.shape[2], out.shape[2]
    per_col, per_row, per_band = side // own, side // piece, BAND // piece
    total[...] = jnp.zeros_like(total)
    for k in range(slots):
        live, row, col, scale = slot_info(info, k, slots)
        for j in range(side // BAND):
            loads[k, j].wait()

            @pl.when(live)
            def _(j=j, k=k, row=row, col=col, scale=scale):
                panel = jnp.concatenate([panels[col * per_col + i] for i in range(per_col)], axis=1)
                product = scale * lax.dot_general(
                    panel,
                    held[k, pl.ds(BAND * j, BAND), :],
                    (((1,), (1,)), ((), ())),
                    preferred_element_type=jnp.float32,
                )
                for t in range(per_band):
                    where = row * per_row + j * per_band + t
                    total[where] = total[where] + product[:, t * piece : (t + 1) * piece]

    for c in range(out.shape[0]):
        encode(total[c], out, (c,))


def partial_kernel(coded, out):
    encode(decode(coded), out, (0,))
    for i in range(1, out.shape[0]):
        out[i] = out[0]


def weigh_kernel(coded, noise, out):
    here = lax.axis_index(NEAR)
    weighted = (noise[pl.ds(here, 1), :] * decode(coded)).astype(jnp.bfloat16)
    for i in range(out.shape[0]):
        out[i] = weighted


def back_kernel(info, weighted, held, out, total):
    slots, side, _ = held.shape
    piece, own = weighted.shape[2], out.shape[2]
    per_col, per_row = side // own, side // piece
    total[...] = jnp.zeros_like(total)
    for k in range(slots):
        live, row, col, scale = slot_info(info, k, slots)

        @pl.when(live)
        def _(k=k, row=row, col=col, scale=scale):
            rows = jnp.concatenate([weighted[row * per_row + i] for i in range(per_row)], axis=1)
            for t in range(per_col):
                product = scale * jnp.dot(
                    rows, held[k, :, pl.ds(own * t, own)], preferred_element_type=jnp.float32
                )
                where = col * per_col + t
                total[where] = total[where] + product

    out[...] = total[...].astype(jnp.bfloat16)


def shards(
    unscaled_tile_values,
    tile_observe_row,
    tile_param_block,
    tile_scale_exponent,
    tile_count,
    probes,
    noise_weight,
):
    own, width = probes.shape
    n_obs = lax.axis_size(OBS)
    n_near = lax.axis_size(NEAR)
    piece = noise_weight.shape[0] // n_near
    slots, _, side, _ = unscaled_tile_values.shape
    bf16, f32 = jnp.bfloat16, jnp.float32

    copies, info = call(
        start_kernel,
        (pltpu.VMEM((n_obs, width, own), bf16), pltpu.SMEM((1 + 3 * slots,), jnp.int32)),
        [SMEM] + [HBM] * 4,
        tile_count,
        in_hbm(tile_observe_row.T),
        in_hbm(tile_param_block.T),
        in_hbm(tile_scale_exponent.T),
        in_hbm(probes.T),
        out_specs=(VMEM, SMEM),
        scratch=[
            pltpu.SMEM((3, 1, slots), jnp.int32),
            pltpu.SemaphoreType.DMA((n_obs,)),
            pltpu.SemaphoreType.DMA((3,)),
        ],
    )
    panels = exchange(copies, OBS)
    coded = width + SCALE_ROWS
    pieces, held = call(
        forward_kernel,
        (pltpu.VMEM((n_near, coded, piece), CODE), pltpu.VMEM((slots, side, side), bf16)),
        [SMEM, VMEM, HBM],
        info,
        panels,
        in_hbm(unscaled_tile_values),
        out_specs=(VMEM, VMEM),
        scratch=[
            pltpu.VMEM((n_near, width, piece), f32),
            pltpu.SemaphoreType.DMA((slots, side // BAND)),
        ],
    )
    partial = call(
        partial_kernel,
        pltpu.VMEM((lax.axis_size("zh"), coded, piece), CODE),
        [VMEM],
        exchange(pieces, NEAR),
    )
    weighted = call(
        weigh_kernel,
        pltpu.VMEM((n_near, width, piece), bf16),
        [VMEM] * 2,
        exchange(partial, "zh"),
        noise_weight.reshape(n_near, piece),
    )
    weighted = exchange(weighted, NEAR)
    pieces = call(
        back_kernel,
        pltpu.VMEM((n_obs, width, own), bf16),
        [SMEM, VMEM, VMEM],
        info,
        weighted,
        held,
        scratch=[pltpu.VMEM((n_obs, width, own), f32)],
    )
    summed = exchange(pieces, OBS).astype(f32).sum(0)
    return summed.T


def solution(mesh):
    n_par, n_obs = mesh.devices.shape
    devices = mesh.devices.reshape(4, n_par // 16, 4, n_obs // 2, 2)
    split = Mesh(devices, PAR + OBS)
    in_specs = (
        P(PAR, OBS, None, None),
        P(PAR, OBS),
        P(PAR, OBS),
        P(PAR, OBS),
        P(PAR, OBS),
        P(PAR + OBS, None),
        P(OBS),
    )
    out_specs = P(PAR + OBS, None)
    return jax.shard_map(shards, mesh=split, in_specs=in_specs, out_specs=out_specs, check_vma=False)
```

```python
import jax
import jax.numpy as jnp
from jax import lax
from jax.experimental import pallas as pl
from jax.experimental.pallas import tpu as pltpu
from jax.sharding import Mesh, PartitionSpec as P

OBS = ("y", "core")
PAR = ("x", "zh", "zl")
NEAR = ("x", "zl")
VMEM = pl.BlockSpec(memory_space=pltpu.VMEM)
SMEM = pl.BlockSpec(memory_space=pltpu.SMEM)
HBM = pl.BlockSpec(memory_space=pltpu.HBM)
PARAMS = pltpu.CompilerParams(vmem_limit_bytes=16 * 2**20)
BAND = 256
FIRST_PANELS, FIRST_NEAR, FIRST_FAR, FIRST_WEIGHTED, FIRST_LAST = 7, 10, 2, 10, 1
CODE = jnp.int16
SCALE_ROWS = 8


def exchange(pieces, axes, first):
    groups = [[i ^ first for i in range(pieces.shape[0])]]
    return lax.all_to_all(pieces, axes, 0, 0, tiled=True, axis_index_groups=groups)


def in_hbm(array):
    return pltpu.with_memory_space_constraint(array, pltpu.HBM)


def call(kernel, out, in_specs, *args, out_specs=VMEM, scratch=()):
    return pl.pallas_call(
        kernel,
        out_shape=out,
        in_specs=in_specs,
        out_specs=out_specs,
        scratch_shapes=list(scratch),
        compiler_params=PARAMS,
    )(*args)


def power(exponent):
    return lax.shift_left(jnp.int32(1), exponent + 1).astype(jnp.float32) * 0.5


def start_kernel(count, row, col, exponent, probes, copies, info, held, arrived, read):
    sent = [
        pltpu.make_async_copy(probes, copies.at[i], arrived.at[i]) for i in range(copies.shape[0])
    ]
    sent += [
        pltpu.make_async_copy(source, held.at[i], read.at[i])
        for i, source in enumerate((row, col, exponent))
    ]
    for copy in sent:
        copy.start()
    for copy in sent:
        copy.wait()
    slots = row.shape[1]
    info[0] = count[0, 0]
    for i in range(3):
        for k in range(slots):
            info[1 + i * slots + k] = held[i, 0, k]


def encode(values, out, at):
    rows = values.shape[0]
    largest = jnp.max(jnp.abs(values), axis=0, keepdims=True)
    exponent = jnp.floor(jnp.log2(jnp.maximum(largest, 2.0**-110))) + 1.0
    codes = jnp.round(values * jnp.exp2(14.0 - exponent))
    exponent = jnp.broadcast_to(exponent, (SCALE_ROWS, values.shape[1]))
    both = jnp.concatenate([codes, exponent], axis=0)
    out[at] = both.astype(jnp.int32).astype(CODE)


def decode(coded):
    pieces, rows, _ = coded.shape
    rows -= SCALE_ROWS
    total = None
    for i in range(pieces):
        both = coded[i].astype(jnp.float32)
        part = both[:rows] * jnp.exp2(both[rows : rows + 1] - 14.0)
        total = part if total is None else total + part
    return total


def slot_info(info, k, slots):
    scale = power(info[1 + 2 * slots + k])
    return k < info[0], info[1 + k], info[1 + slots + k], scale


def load_bands(tiles, held, arrived):
    slots, _, side, _ = tiles.shape
    loads = {}
    for k in range(slots):
        for j in range(side // BAND):
            band = pl.ds(BAND * j, BAND)
            loads[k, j] = pltpu.make_async_copy(
                tiles.at[k, 0, band], held.at[k, band], arrived.at[k, j]
            )
            loads[k, j].start()
    return loads


def forward_kernel(info, panels, tiles, out, held, total, arrived):
    loads = load_bands(tiles, held, arrived)
    slots, side, _ = held.shape
    own, piece = panels.shape[2], out.shape[2]
    per_col, per_row, per_band = side // own, side // piece, BAND // piece
    total[...] = jnp.zeros_like(total)
    for k in range(slots):
        live, row, col, scale = slot_info(info, k, slots)
        for j in range(side // BAND):
            loads[k, j].wait()

            @pl.when(live)
            def _(j=j, k=k, row=row, col=col, scale=scale):
                panel = jnp.concatenate([panels[(col * per_col + i) ^ FIRST_PANELS] for i in range(per_col)], axis=1)
                product = scale * lax.dot_general(
                    panel,
                    held[k, pl.ds(BAND * j, BAND), :],
                    (((1,), (1,)), ((), ())),
                    preferred_element_type=jnp.float32,
                )
                for t in range(per_band):
                    where = row * per_row + j * per_band + t
                    total[where] = total[where] + product[:, t * piece : (t + 1) * piece]

    for c in range(out.shape[0]):
        encode(total[c], out, c ^ FIRST_NEAR)


def partial_kernel(coded, out):
    encode(decode(coded), out, 0)
    for i in range(1, out.shape[0]):
        out[i] = out[0]


def weigh_kernel(coded, noise, out):
    here = lax.axis_index(NEAR)
    weighted = (noise[pl.ds(here, 1), :] * decode(coded)).astype(jnp.bfloat16)
    for i in range(out.shape[0]):
        out[i] = weighted


def back_kernel(info, weighted, held, out, total):
    slots, side, _ = held.shape
    piece, own = weighted.shape[2], out.shape[2]
    per_col, per_row = side // own, side // piece
    total[...] = jnp.zeros_like(total)
    for k in range(slots):
        live, row, col, scale = slot_info(info, k, slots)

        @pl.when(live)
        def _(k=k, row=row, col=col, scale=scale):
            rows = jnp.concatenate([weighted[(row * per_row + i) ^ FIRST_WEIGHTED] for i in range(per_row)], axis=1)
            for t in range(per_col):
                product = scale * jnp.dot(
                    rows, held[k, :, pl.ds(own * t, own)], preferred_element_type=jnp.float32
                )
                where = col * per_col + t
                total[where] = total[where] + product

    for o in range(out.shape[0]):
        out[o ^ FIRST_LAST] = total[o].astype(jnp.bfloat16)


def shards(
    unscaled_tile_values,
    tile_observe_row,
    tile_param_block,
    tile_scale_exponent,
    tile_count,
    probes,
    noise_weight,
):
    own, width = probes.shape
    n_obs = lax.axis_size(OBS)
    n_near = lax.axis_size(NEAR)
    piece = noise_weight.shape[0] // n_near
    slots, _, side, _ = unscaled_tile_values.shape
    bf16, f32 = jnp.bfloat16, jnp.float32

    copies, info = call(
        start_kernel,
        (pltpu.VMEM((n_obs, width, own), bf16), pltpu.SMEM((1 + 3 * slots,), jnp.int32)),
        [SMEM] + [HBM] * 4,
        tile_count,
        in_hbm(tile_observe_row.T),
        in_hbm(tile_param_block.T),
        in_hbm(tile_scale_exponent.T),
        in_hbm(probes.T),
        out_specs=(VMEM, SMEM),
        scratch=[
            pltpu.SMEM((3, 1, slots), jnp.int32),
            pltpu.SemaphoreType.DMA((n_obs,)),
            pltpu.SemaphoreType.DMA((3,)),
        ],
    )
    panels = exchange(copies, OBS, FIRST_PANELS)
    coded = width + SCALE_ROWS
    pieces, held = call(
        forward_kernel,
        (pltpu.VMEM((n_near, coded, piece), CODE), pltpu.VMEM((slots, side, side), bf16)),
        [SMEM, VMEM, HBM],
        info,
        panels,
        in_hbm(unscaled_tile_values),
        out_specs=(VMEM, VMEM),
        scratch=[
            pltpu.VMEM((n_near, width, piece), f32),
            pltpu.SemaphoreType.DMA((slots, side // BAND)),
        ],
    )
    partial = call(
        partial_kernel,
        pltpu.VMEM((lax.axis_size("zh"), coded, piece), CODE),
        [VMEM],
        exchange(pieces, NEAR, FIRST_NEAR),
    )
    weighted = call(
        weigh_kernel,
        pltpu.VMEM((n_near, width, piece), bf16),
        [VMEM] * 2,
        exchange(partial, "zh", FIRST_FAR),
        noise_weight.reshape(n_near, piece),
    )
    weighted = exchange(weighted, NEAR, FIRST_WEIGHTED)
    pieces = call(
        back_kernel,
        pltpu.VMEM((n_obs, width, own), bf16),
        [SMEM, VMEM, VMEM],
        info,
        weighted,
        held,
        scratch=[pltpu.VMEM((n_obs, width, own), f32)],
    )
    summed = exchange(pieces, OBS, FIRST_LAST).astype(f32).sum(0)
    return summed.T


def solution(mesh):
    n_par, n_obs = mesh.devices.shape
    devices = mesh.devices.reshape(4, n_par // 16, 4, n_obs // 2, 2)
    split = Mesh(devices, PAR + OBS)
    in_specs = (
        P(PAR, OBS, None, None),
        P(PAR, OBS),
        P(PAR, OBS),
        P(PAR, OBS),
        P(PAR, OBS),
        P(PAR + OBS, None),
        P(OBS),
    )
    out_specs = P(PAR + OBS, None)
    return jax.shard_map(shards, mesh=split, in_specs=in_specs, out_specs=out_specs, check_vma=False)
```

```python
import jax
import jax.numpy as jnp
from jax import lax
from jax.experimental import pallas as pl
from jax.experimental.pallas import tpu as pltpu
from jax.sharding import Mesh, PartitionSpec as P

OBS = ("y", "core")
PAR = ("x", "zh", "zl")
NEAR = ("x", "zl")
VMEM = pl.BlockSpec(memory_space=pltpu.VMEM)
SMEM = pl.BlockSpec(memory_space=pltpu.SMEM)
HBM = pl.BlockSpec(memory_space=pltpu.HBM)
PARAMS = pltpu.CompilerParams(vmem_limit_bytes=16 * 2**20)
BAND = 512
FIRST_PANELS, FIRST_NEAR, FIRST_FAR, FIRST_WEIGHTED, FIRST_LAST = 7, 10, 2, 10, 5
CODE = jnp.int16
SCALE_ROWS = 8


def exchange(pieces, axes, first):
    groups = [[i ^ first for i in range(pieces.shape[0])]]
    return lax.all_to_all(pieces, axes, 0, 0, tiled=True, axis_index_groups=groups)


def in_hbm(array):
    return pltpu.with_memory_space_constraint(array, pltpu.HBM)


def call(kernel, out, in_specs, *args, out_specs=VMEM, scratch=()):
    return pl.pallas_call(
        kernel,
        out_shape=out,
        in_specs=in_specs,
        out_specs=out_specs,
        scratch_shapes=list(scratch),
        compiler_params=PARAMS,
    )(*args)


def power(exponent):
    return lax.shift_left(jnp.int32(1), exponent + 1).astype(jnp.float32) * 0.5


def start_kernel(count, row, col, exponent, probes, copies, info, held, arrived, read):
    sent = [
        pltpu.make_async_copy(probes, copies.at[i], arrived.at[i]) for i in range(copies.shape[0])
    ]
    sent += [
        pltpu.make_async_copy(source, held.at[i], read.at[i])
        for i, source in enumerate((row, col, exponent))
    ]
    for copy in sent:
        copy.start()
    for copy in sent:
        copy.wait()
    slots = row.shape[1]
    info[0] = count[0, 0]
    for i in range(3):
        for k in range(slots):
            info[1 + i * slots + k] = held[i, 0, k]


def encode(values, out, at):
    rows = values.shape[0]
    largest = jnp.max(jnp.abs(values), axis=0, keepdims=True)
    exponent = jnp.floor(jnp.log2(jnp.maximum(largest, 2.0**-110))) + 1.0
    codes = jnp.round(values * jnp.exp2(14.0 - exponent))
    exponent = jnp.broadcast_to(exponent, (SCALE_ROWS, values.shape[1]))
    both = jnp.concatenate([codes, exponent], axis=0)
    out[at] = both.astype(jnp.int32).astype(CODE)


def decode(coded):
    pieces, rows, _ = coded.shape
    rows -= SCALE_ROWS
    total = None
    for i in range(pieces):
        both = coded[i].astype(jnp.float32)
        part = both[:rows] * jnp.exp2(both[rows : rows + 1] - 14.0)
        total = part if total is None else total + part
    return total


def slot_info(info, k, slots):
    scale = power(info[1 + 2 * slots + k])
    return k < info[0], info[1 + k], info[1 + slots + k], scale


def load_bands(tiles, held, arrived):
    slots, _, side, _ = tiles.shape
    loads = {}
    for k in range(slots):
        for j in range(side // BAND):
            band = pl.ds(BAND * j, BAND)
            loads[k, j] = pltpu.make_async_copy(
                tiles.at[k, 0, band], held.at[k, band], arrived.at[k, j]
            )
            loads[k, j].start()
    return loads


def forward_kernel(info, panels, tiles, out, held, total, arrived):
    loads = load_bands(tiles, held, arrived)
    slots, side, _ = held.shape
    own, piece = panels.shape[2], out.shape[2]
    per_col, per_row, per_band = side // own, side // piece, BAND // piece
    total[...] = jnp.zeros_like(total)
    for k in range(slots):
        live, row, col, scale = slot_info(info, k, slots)
        for j in range(side // BAND):
            loads[k, j].wait()

            @pl.when(live)
            def _(j=j, k=k, row=row, col=col, scale=scale):
                panel = jnp.concatenate([panels[(col * per_col + i) ^ FIRST_PANELS] for i in range(per_col)], axis=1)
                product = scale * lax.dot_general(
                    panel,
                    held[k, pl.ds(BAND * j, BAND), :],
                    (((1,), (1,)), ((), ())),
                    preferred_element_type=jnp.float32,
                )
                for t in range(per_band):
                    where = row * per_row + j * per_band + t
                    total[where] = total[where] + product[:, t * piece : (t + 1) * piece]

    for c in range(out.shape[0]):
        encode(total[c], out, c ^ FIRST_NEAR)


def partial_kernel(coded, out):
    encode(decode(coded), out, 0)
    for i in range(1, out.shape[0]):
        out[i] = out[0]


def weigh_kernel(coded, noise, out):
    here = lax.axis_index(NEAR)
    weighted = (noise[pl.ds(here, 1), :] * decode(coded)).astype(jnp.bfloat16)
    for i in range(out.shape[0]):
        out[i] = weighted


def back_kernel(info, weighted, held, out, total):
    slots, side, _ = held.shape
    piece, own = weighted.shape[2], out.shape[2]
    per_col, per_row = side // own, side // piece
    total[...] = jnp.zeros_like(total)
    for k in range(slots):
        live, row, col, scale = slot_info(info, k, slots)

        @pl.when(live)
        def _(k=k, row=row, col=col, scale=scale):
            rows = jnp.concatenate([weighted[(row * per_row + i) ^ FIRST_WEIGHTED] for i in range(per_row)], axis=1)
            for t in range(per_col):
                product = scale * jnp.dot(
                    rows, held[k, :, pl.ds(own * t, own)], preferred_element_type=jnp.float32
                )
                where = col * per_col + t
                total[where] = total[where] + product

    for o in range(out.shape[0]):
        out[o ^ FIRST_LAST] = total[o].astype(jnp.bfloat16)


def shards(
    unscaled_tile_values,
    tile_observe_row,
    tile_param_block,
    tile_scale_exponent,
    tile_count,
    probes,
    noise_weight,
):
    own, width = probes.shape
    n_obs = lax.axis_size(OBS)
    n_near = lax.axis_size(NEAR)
    piece = noise_weight.shape[0] // n_near
    slots, _, side, _ = unscaled_tile_values.shape
    bf16, f32 = jnp.bfloat16, jnp.float32

    copies, info = call(
        start_kernel,
        (pltpu.VMEM((n_obs, width, own), bf16), pltpu.SMEM((1 + 3 * slots,), jnp.int32)),
        [SMEM] + [HBM] * 4,
        tile_count,
        in_hbm(tile_observe_row.T),
        in_hbm(tile_param_block.T),
        in_hbm(tile_scale_exponent.T),
        in_hbm(probes.T),
        out_specs=(VMEM, SMEM),
        scratch=[
            pltpu.SMEM((3, 1, slots), jnp.int32),
            pltpu.SemaphoreType.DMA((n_obs,)),
            pltpu.SemaphoreType.DMA((3,)),
        ],
    )
    panels = exchange(copies, OBS, FIRST_PANELS)
    coded = width + SCALE_ROWS
    pieces, held = call(
        forward_kernel,
        (pltpu.VMEM((n_near, coded, piece), CODE), pltpu.VMEM((slots, side, side), bf16)),
        [SMEM, VMEM, HBM],
        info,
        panels,
        in_hbm(unscaled_tile_values),
        out_specs=(VMEM, VMEM),
        scratch=[
            pltpu.VMEM((n_near, width, piece), f32),
            pltpu.SemaphoreType.DMA((slots, side // BAND)),
        ],
    )
    partial = call(
        partial_kernel,
        pltpu.VMEM((lax.axis_size("zh"), coded, piece), CODE),
        [VMEM],
        exchange(pieces, NEAR, FIRST_NEAR),
    )
    weighted = call(
        weigh_kernel,
        pltpu.VMEM((n_near, width, piece), bf16),
        [VMEM] * 2,
        exchange(partial, "zh", FIRST_FAR),
        noise_weight.reshape(n_near, piece),
    )
    weighted = exchange(weighted, NEAR, FIRST_WEIGHTED)
    pieces = call(
        back_kernel,
        pltpu.VMEM((n_obs, width, own), bf16),
        [SMEM, VMEM, VMEM],
        info,
        weighted,
        held,
        scratch=[pltpu.VMEM((n_obs, width, own), f32)],
    )
    summed = exchange(pieces, OBS, FIRST_LAST).astype(f32).sum(0)
    return summed.T


def solution(mesh):
    n_par, n_obs = mesh.devices.shape
    devices = mesh.devices.reshape(4, n_par // 16, 4, n_obs // 2, 2)
    split = Mesh(devices, PAR + OBS)
    in_specs = (
        P(PAR, OBS, None, None),
        P(PAR, OBS),
        P(PAR, OBS),
        P(PAR, OBS),
        P(PAR, OBS),
        P(PAR + OBS, None),
        P(OBS),
    )
    out_specs = P(PAR + OBS, None)
    return jax.shard_map(shards, mesh=split, in_specs=in_specs, out_specs=out_specs, check_vma=False)
```

```python
import jax
import jax.numpy as jnp
from jax import lax
from jax.experimental import pallas as pl
from jax.experimental.pallas import tpu as pltpu
from jax.sharding import Mesh, PartitionSpec as P

OBS = ("y", "core")
PAR = ("x", "zh", "zl")
NEAR = ("x", "zl")
VMEM = pl.BlockSpec(memory_space=pltpu.VMEM)
SMEM = pl.BlockSpec(memory_space=pltpu.SMEM)
HBM = pl.BlockSpec(memory_space=pltpu.HBM)
PARAMS = pltpu.CompilerParams(vmem_limit_bytes=16 * 2**20)
BAND = 512
FIRST_PANELS, FIRST_NEAR, FIRST_FAR, FIRST_WEIGHTED, FIRST_LAST = 7, 10, 2, 10, 5
CODE = jnp.int16
SCALE_ROWS = 8


def exchange(pieces, axes, first):
    groups = [[i ^ first for i in range(pieces.shape[0])]]
    return lax.all_to_all(pieces, axes, 0, 0, tiled=True, axis_index_groups=groups)


def in_hbm(array):
    return pltpu.with_memory_space_constraint(array, pltpu.HBM)


def call(kernel, out, in_specs, *args, out_specs=VMEM, scratch=()):
    return pl.pallas_call(
        kernel,
        out_shape=out,
        in_specs=in_specs,
        out_specs=out_specs,
        scratch_shapes=list(scratch),
        compiler_params=PARAMS,
    )(*args)


def power(exponent):
    return lax.shift_left(jnp.int32(1), exponent + 1).astype(jnp.float32) * 0.5


def start_kernel(count, row, col, exponent, probes, copies, info, held, arrived, read):
    sent = [pltpu.make_async_copy(probes, copies.at[0], arrived.at[0])]
    sent += [
        pltpu.make_async_copy(source, held.at[i], read.at[i])
        for i, source in enumerate((row, col, exponent))
    ]
    for copy in sent:
        copy.start()
    for copy in sent:
        copy.wait()
    for i in range(1, copies.shape[0]):
        copies[i] = copies[0]
    slots = row.shape[1]
    info[0] = count[0, 0]
    for i in range(3):
        for k in range(slots):
            info[1 + i * slots + k] = held[i, 0, k]


def encode(values, out, at):
    rows = values.shape[0]
    largest = jnp.max(jnp.abs(values), axis=0, keepdims=True)
    exponent = jnp.floor(jnp.log2(jnp.maximum(largest, 2.0**-110))) + 1.0
    codes = jnp.round(values * jnp.exp2(14.0 - exponent))
    exponent = jnp.broadcast_to(exponent, (SCALE_ROWS, values.shape[1]))
    both = jnp.concatenate([codes, exponent], axis=0)
    out[at] = both.astype(jnp.int32).astype(CODE)


def decode(coded):
    pieces, rows, _ = coded.shape
    rows -= SCALE_ROWS
    total = None
    for i in range(pieces):
        both = coded[i].astype(jnp.float32)
        part = both[:rows] * jnp.exp2(both[rows : rows + 1] - 14.0)
        total = part if total is None else total + part
    return total


def slot_info(info, k, slots):
    scale = power(info[1 + 2 * slots + k])
    return k < info[0], info[1 + k], info[1 + slots + k], scale


def load_bands(tiles, held, arrived):
    slots, _, side, _ = tiles.shape
    loads = {}
    for k in range(slots):
        for j in range(side // BAND):
            band = pl.ds(BAND * j, BAND)
            loads[k, j] = pltpu.make_async_copy(
                tiles.at[k, 0, band], held.at[k, band], arrived.at[k, j]
            )
            loads[k, j].start()
    return loads


def forward_kernel(info, panels, tiles, out, held, total, arrived):
    loads = load_bands(tiles, held, arrived)
    slots, side, _ = held.shape
    own, piece = panels.shape[2], out.shape[2]
    per_col, per_row, per_band = side // own, side // piece, BAND // piece
    total[...] = jnp.zeros_like(total)
    for k in range(slots):
        live, row, col, scale = slot_info(info, k, slots)
        for j in range(side // BAND):
            loads[k, j].wait()

            @pl.when(live)
            def _(j=j, k=k, row=row, col=col, scale=scale):
                panel = jnp.concatenate([panels[(col * per_col + i) ^ FIRST_PANELS] for i in range(per_col)], axis=1)
                product = scale * lax.dot_general(
                    panel,
                    held[k, pl.ds(BAND * j, BAND), :],
                    (((1,), (1,)), ((), ())),
                    preferred_element_type=jnp.float32,
                )
                for t in range(per_band):
                    where = row * per_row + j * per_band + t
                    total[where] = total[where] + product[:, t * piece : (t + 1) * piece]

    for c in range(out.shape[0]):
        encode(total[c], out, c ^ FIRST_NEAR)


def partial_kernel(coded, out):
    encode(decode(coded), out, 0)
    for i in range(1, out.shape[0]):
        out[i] = out[0]


def weigh_kernel(coded, noise, out):
    here = lax.axis_index(NEAR)
    weighted = (noise[pl.ds(here, 1), :] * decode(coded)).astype(jnp.bfloat16)
    for i in range(out.shape[0]):
        out[i] = weighted


def back_kernel(info, weighted, held, out, total):
    slots, side, _ = held.shape
    piece, own = weighted.shape[2], out.shape[2]
    per_col, per_row = side // own, side // piece
    total[...] = jnp.zeros_like(total)
    for k in range(slots):
        live, row, col, scale = slot_info(info, k, slots)

        @pl.when(live)
        def _(k=k, row=row, col=col, scale=scale):
            rows = jnp.concatenate([weighted[(row * per_row + i) ^ FIRST_WEIGHTED] for i in range(per_row)], axis=1)
            for t in range(per_col):
                product = scale * jnp.dot(
                    rows, held[k, :, pl.ds(own * t, own)], preferred_element_type=jnp.float32
                )
                where = col * per_col + t
                total[where] = total[where] + product

    for o in range(out.shape[0]):
        out[o ^ FIRST_LAST] = total[o].astype(jnp.bfloat16)


def shards(
    unscaled_tile_values,
    tile_observe_row,
    tile_param_block,
    tile_scale_exponent,
    tile_count,
    probes,
    noise_weight,
):
    own, width = probes.shape
    n_obs = lax.axis_size(OBS)
    n_near = lax.axis_size(NEAR)
    piece = noise_weight.shape[0] // n_near
    slots, _, side, _ = unscaled_tile_values.shape
    bf16, f32 = jnp.bfloat16, jnp.float32

    copies, info = call(
        start_kernel,
        (pltpu.VMEM((n_obs, width, own), bf16), pltpu.SMEM((1 + 3 * slots,), jnp.int32)),
        [SMEM] + [HBM] * 4,
        tile_count,
        in_hbm(tile_observe_row.T),
        in_hbm(tile_param_block.T),
        in_hbm(tile_scale_exponent.T),
        in_hbm(probes.T),
        out_specs=(VMEM, SMEM),
        scratch=[
            pltpu.SMEM((3, 1, slots), jnp.int32),
            pltpu.SemaphoreType.DMA((n_obs,)),
            pltpu.SemaphoreType.DMA((3,)),
        ],
    )
    panels = exchange(copies, OBS, FIRST_PANELS)
    coded = width + SCALE_ROWS
    pieces, held = call(
        forward_kernel,
        (pltpu.VMEM((n_near, coded, piece), CODE), pltpu.VMEM((slots, side, side), bf16)),
        [SMEM, VMEM, HBM],
        info,
        panels,
        in_hbm(unscaled_tile_values),
        out_specs=(VMEM, VMEM),
        scratch=[
            pltpu.VMEM((n_near, width, piece), f32),
            pltpu.SemaphoreType.DMA((slots, side // BAND)),
        ],
    )
    partial = call(
        partial_kernel,
        pltpu.VMEM((lax.axis_size("zh"), coded, piece), CODE),
        [VMEM],
        exchange(pieces, NEAR, FIRST_NEAR),
    )
    weighted = call(
        weigh_kernel,
        pltpu.VMEM((n_near, width, piece), bf16),
        [VMEM] * 2,
        exchange(partial, "zh", FIRST_FAR),
        noise_weight.reshape(n_near, piece),
    )
    weighted = exchange(weighted, NEAR, FIRST_WEIGHTED)
    pieces = call(
        back_kernel,
        pltpu.VMEM((n_obs, width, own), bf16),
        [SMEM, VMEM, VMEM],
        info,
        weighted,
        held,
        scratch=[pltpu.VMEM((n_obs, width, own), f32)],
    )
    summed = exchange(pieces, OBS, FIRST_LAST).astype(f32).sum(0)
    return summed.T


def solution(mesh):
    n_par, n_obs = mesh.devices.shape
    devices = mesh.devices.reshape(4, n_par // 16, 4, n_obs // 2, 2)
    split = Mesh(devices, PAR + OBS)
    in_specs = (
        P(PAR, OBS, None, None),
        P(PAR, OBS),
        P(PAR, OBS),
        P(PAR, OBS),
        P(PAR, OBS),
        P(PAR + OBS, None),
        P(OBS),
    )
    out_specs = P(PAR + OBS, None)
    return jax.shard_map(shards, mesh=split, in_specs=in_specs, out_specs=out_specs, check_vma=False)
```
